256 devices in a mesh: owner: 64 (over z, y, core), aux: 4 (over x).
Axes of the slice: x: 4, y: 4, z: 8, core: 2. Of those that a mesh axis runs over, the one named last changes fastest.
Arguments:
- blocks: bfloat16 [256, 256, 2048], P('owner', None, 'aux'), may hold values from -0.890625 to 0.890625
- wanted: int32 [64, 64, 1], P('owner'), may hold values from 0 to 3
- pair_local: int32 [64, 64], P('owner'), may hold values from 0 to 3
- pair_slot: int32 [64, 64], P('owner'), may hold values from 0 to 63, each once within a row
- pno_local: bfloat16 [64, 64, 256, 128], P('owner'), may hold values from -0.375 to 0.375
- pno_remote: bfloat16 [64, 64, 256, 128], P('owner'), may hold values from -0.375 to 0.375
Outputs:
- integrals: bfloat16 [64, 64, 128, 128], P('owner', 'aux')
The draws below stay inside these ranges and needn't reach their ends.
Inputs may be any that keep to these rules, and one draw needn't show every extreme that they name: pair_slot is a permutation of the requests of each owner.
All inputs are finite; a program needn't handle non-finite values.
Results may differ from the reference program's by a relative error of at most 0.0057.
Values may be sent and summed in bfloat16 or wider, within the bound.
A program may use at most 128 MiB of HBM per device.

```python
import jax
import jax.numpy as jnp
from jax import lax

DOM = 256
NAUX = 2048
NPNO = 128
OCC_DEV = 4
CAP = 1
SLOTS = 64
OCC = 256
N_OWNER = 64


def set_ends(array, stream_key, smallest, high):
    index_at = [jax.random.randint(jax.random.fold_in(stream_key, axis), (), 0, length) for axis, length in enumerate(array.shape)]
    longest = array.shape.index(max(array.shape))
    next_to = index_at[:longest] + [(index_at[longest] + 1) % array.shape[longest]] + index_at[longest + 1:]
    return array.at[tuple(index_at)].set(smallest).at[tuple(next_to)].set(high)


def level_of(key, dims, cuts, smallest, high):
    loudness = 1.0
    for axis_at, shards_of in cuts:
        steps = jax.random.uniform(jax.random.fold_in(jax.random.fold_in(key, 6), axis_at), (shards_of,), jnp.float32, smallest / len(cuts), high / len(cuts))
        loudness = loudness * jnp.repeat(jnp.exp(steps), dims[axis_at] // shards_of).reshape((-1,) + (1,) * (len(dims) - 1 - axis_at))
    return loudness


def scatter_about(key, extent, spread, reach, shards=(), kind=jnp.bfloat16):
    gain = level_of(key, extent, shards, -0.22, 0.18) if shards else 1.0
    entries = jax.random.normal(key, extent, jnp.float32) * spread * gain
    return jnp.minimum(jnp.maximum(entries, -reach), reach).astype(kind)


def setup_inputs(seed: int = 0) -> dict:
    streams_of = jax.random.split(jax.random.key(seed), 7)
    return {
        "blocks": scatter_about(streams_of[0], (OCC, DOM, NAUX), (NAUX ** -0.25), 0.890625, ((0, 64), (2, 4))),
        "wanted": set_ends(jax.random.randint(streams_of[1], (N_OWNER, N_OWNER, CAP), 0, OCC_DEV), jax.random.fold_in(streams_of[1], 1), 0, OCC_DEV - 1).astype(jnp.int32),
        "pair_local": set_ends(jax.random.randint(streams_of[2], (N_OWNER, SLOTS), 0, OCC_DEV), jax.random.fold_in(streams_of[2], 1), 0, OCC_DEV - 1).astype(jnp.int32),
        "pair_slot": jax.vmap(lambda own: jax.random.permutation(own, SLOTS))(jax.random.split(streams_of[3], N_OWNER)).reshape((N_OWNER, SLOTS)).astype(jnp.int32),
        "pno_local": scatter_about(streams_of[4], (N_OWNER, SLOTS, DOM, NPNO), DOM ** -0.5, 0.375, ((0, 64),)),
        "pno_remote": scatter_about(streams_of[5], (N_OWNER, SLOTS, DOM, NPNO), DOM ** -0.5, 0.375, ((0, 64),)),
    }


def reference(blocks, wanted, pair_local, pair_slot, pno_local, pno_remote):
    def one_owner(args):
        owner_index, wanted_row, local_row, slot_row, maps_local, maps_remote = args
        slots = jnp.arange(SLOTS, dtype=jnp.int32)
        requested = (slots // CAP) * OCC_DEV + wanted_row.reshape(-1)
        first = owner_index * OCC_DEV + local_row
        first_blocks = jnp.take(blocks, first, axis=0).astype(jnp.float32)
        second_blocks = jnp.take(blocks, requested, axis=0).astype(jnp.float32)
        left = jnp.einsum("pdk,pdq->pkq", maps_local.astype(jnp.float32), first_blocks).astype(jnp.bfloat16)
        right = jnp.einsum("pdk,pdq->pkq", maps_remote.astype(jnp.float32), second_blocks).astype(jnp.bfloat16)
        right = jnp.take(right, slot_row, axis=0)
        result = jnp.einsum("pkq,plq->pkl", left.astype(jnp.float32), right.astype(jnp.float32))
        return result.astype(jnp.bfloat16)

    owners = jnp.arange(N_OWNER, dtype=jnp.int32)
    return lax.map(one_owner, (owners, wanted, pair_local, pair_slot, pno_local, pno_remote))
```

```python
import functools

import jax
import jax.numpy as jnp
from jax import lax
from jax.experimental import pallas as pl
from jax.experimental.pallas import tpu as pltpu
from jax.sharding import PartitionSpec as P

NX, NY, NZ = 4, 4, 8
PLANE = NY * 2
PAIRS = 64
BF16, F32, I32 = jnp.bfloat16, jnp.float32, jnp.int32
MESH = pl.DeviceIdType.MESH
OFFSETS = (0, -1, 1, -2, 2, -3, 3, 4)


def dot(a, b, ca, cb):
    return lax.dot_general(a, b, (((ca,), (cb,)), ((), ())), preferred_element_type=F32)


def kernel(
    blocks, pno_remote, pno_local, table, out,
    col0, col1, col2, col3, col4, col5, col6, col7,
    rows, maps, maps_local, tables, tables_s,
    stage_a, got_a, stage_b, got_b, acc, own, t_send, t_got, res,
    z_s, z_r, y_s, y_r, c_s, c_r, q_s, q_r, m_s, m_r, w_s, w_r,
    a_s, a_r, b_s, b_r, t_s, t_r, g_s, g_r, f_s, f_r, local_s,
):
    cols = (col0, col1, col2, col3, col4, col5, col6, col7)
    me = lax.axis_index("owner")
    x = lax.axis_index("aux")
    z = lax.div(me, PLANE)
    yc = lax.rem(me, PLANE)
    y = lax.div(yc, 2)
    c = lax.rem(yc, 2)

    def around(v, step, n):
        return lax.rem(v + (step + n), n)

    def at(zz, yy, cc):
        return (zz * NY + yy) * 2 + cc

    z_to = [(at(around(z, d, NZ), y, c), x) for d in (1, -1)]
    y_to = [(at(z, around(y, d, NY), c), x) for d in (1, -1)]
    x_to = [(me, around(x, d, NX)) for d in (1, -1)]
    mate = (at(z, y, 1 - c), x)
    peers = [
        (dy, dc, around(y, dy, NY) * 2 + lax.rem(c + dc, 2))
        for dy, dc in ((1, 0), (3, 0), (1, 1), (3, 1), (2, 0), (2, 1), (0, 1))
    ]

    barrier = pltpu.get_barrier_semaphore()
    hello = z_to + x_to + [(z * PLANE + p, x) for _, _, p in peers]
    for device in hello:
        pl.semaphore_signal(barrier, inc=1, device_id=device, device_id_type=MESH)
    pl.semaphore_wait(barrier, len(hello))

    sent = []

    def remote(src, dst, s, r, device):
        return pltpu.make_async_remote_copy(
            src_ref=src, dst_ref=dst, send_sem=s, recv_sem=r, device_id=device, device_id_type=MESH
        )

    def send(src, dst, s, r, device):
        copy = remote(src, dst, s, r, device)
        copy.start()
        sent.append(copy)

    def got(dst, s, r):
        remote(dst, dst, s, r, mate).wait_recv()

    stripe = pl.ds(pl.multiple_of(x * 64, 64), 64)

    local = []

    def copy_in(src, dst):
        copy = pltpu.make_async_copy(src, dst, local_s.at[len(local)])
        copy.start()
        local.append(copy)

    for n, (dy, dc, p) in enumerate(peers):
        send(table, tables.at[yc], w_s.at[n], w_r.at[n], (z * PLANE + p, x))
    for n, (dy, dc, p) in enumerate(peers):
        send(pno_remote.at[:, p, stripe], maps.at[yc, :, stripe], q_s.at[n], q_r.at[n], (z * PLANE + p, x))
    copy_in(pno_remote.at[:, yc, stripe], maps.at[yc, :, stripe])
    copy_in(table, tables.at[yc])
    copy_in(blocks, col0)
    copy_in(blocks, rows.at[yc])
    copy_in(pno_local, maps_local)

    def column(d, h):
        return 7 if h == 4 else 2 * h - 1 + d

    def orbitals(d, h):
        return range(4) if h < 4 else (range(2) if d == 0 else range(2, 4))

    def z_send(d, h, q):
        src = blocks if h == 1 else cols[column(d, h - 1)]
        send(src.at[q], cols[column(d, h)].at[q], z_s.at[d, h - 1, q], z_r.at[d, h - 1, q], z_to[d])

    def z_got(d, h, q):
        got(cols[column(d, h)].at[q], z_s.at[d, h - 1, q], z_r.at[d, h - 1, q])

    def y_from(d, h):
        return around(y, -h if d == 0 else h, NY) * 2 + c

    def y_send(d, h, q):
        src = blocks.at[q] if h == 1 else rows.at[y_from(d, 1), q]
        there = yc if h == 1 else y_from(d, 1)
        send(src, rows.at[there, q], y_s.at[d, h - 1, q], y_r.at[d, h - 1, q], y_to[d])

    def y_got(d, h, q):
        got(rows.at[y_from(d, h), q], y_s.at[d, h - 1, q], y_r.at[d, h - 1, q])

    def c_send(n, who, q):
        src = blocks.at[q] if n == 0 else rows.at[who, q]
        send(src, rows.at[who, q], c_s.at[n, q], c_r.at[n, q], mate)

    for q in range(4):
        for d in range(2):
            z_send(d, 1, q if d == 0 else 3 - q)
            y_send(d, 1, q if d == 0 else 3 - q)
    for q in range(4):
        c_send(0, yc, q)

    def m_half(d, h):
        return pl.ds(4 * h, 4)

    def m_send(d, hop, half):
        who = x if hop == 1 else around(x, -1 if d == 0 else 1, NX)
        there = maps.at[m_half(d, half), :, pl.ds(pl.multiple_of(who * 64, 64), 64)]
        send(there, there, m_s.at[d, hop - 1, half], m_r.at[d, hop - 1, half], x_to[d])

    def m_got(d, hop, half):
        who = around(x, -hop if d == 0 else hop, NX)
        got(
            maps.at[m_half(d, half), :, pl.ds(pl.multiple_of(who * 64, 64), 64)],
            m_s.at[d, hop - 1, half], m_r.at[d, hop - 1, half],
        )

    def peer_from(n):
        dy, dc, _ = peers[n]
        return around(y, -dy, NY) * 2 + lax.rem(c + dc, 2)

    for n in range(7):
        got(tables.at[peer_from(n)], w_s.at[n], w_r.at[n])
        got(maps.at[peer_from(n), :, stripe], q_s.at[n], q_r.at[n])
    for copy in local:
        copy.wait()
    for half in range(2):
        for d in range(2):
            m_send(d, 1, half if d == 0 else 1 - half)
    scalars = pltpu.make_async_copy(tables, tables_s, local_s.at[5])
    scalars.start()
    scalars.wait()

    def z_turn(h):
        for q in range(4):
            for d in range(2):
                o = q if d == 0 else 3 - q
                z_got(d, h, o)
                if o in orbitals(d, h + 1):
                    z_send(d, h + 1, o)

    z_turn(1)
    for q in range(4):
        for d in range(2):
            o = q if d == 0 else 3 - q
            y_got(d, 1, o)
            if q < 2:
                y_send(d, 2, o)
            c_send(1 + d, y_from(d, 1), o)
    for d in range(2):
        m_got(d, 1, d)
        m_send(d, 2, d)
    z_turn(2)
    for q in range(2):
        for d in range(2):
            o = q if d == 0 else 3 - q
            y_got(d, 2, o)
            c_send(3, y_from(d, 2), o)
    for d in range(2):
        m_got(d, 1, 1 - d)
        m_got(d, 2, d)
    for q in range(4):
        got(rows.at[y * 2 + 1 - c, q], c_s.at[0, q], c_r.at[0, q])
        for d in range(2):
            got(rows.at[around(y, -1 if d == 0 else 1, NY) * 2 + 1 - c, q], c_s.at[1 + d, q], c_r.at[1 + d, q])
        got(rows.at[around(y, 2, NY) * 2 + 1 - c, q], c_s.at[3, q], c_r.at[3, q])

    def plane(k):
        return around(z, OFFSETS[k], NZ)

    def row_of(k, dx):
        return lax.rem(x + (dx + 16) - y - plane(k), NY)

    def partial(k, dx, half):
        o = row_of(k, dx) * 2 + half
        s = plane(k) * PLANE + yc
        i = tables_s[o, 1, s]
        j = tables_s[o, 0, s]
        right = dot(maps[o, plane(k)], cols[k][j], 0, 0).astype(BF16)
        return dot(rows[o, i], right, 1, 1)

    def first(k):
        for half in range(2):
            stage_a[k, half] = partial(k, 2, half).astype(BF16)
            send(stage_a.at[k, half], got_a.at[k, half], a_s.at[k, half], a_r.at[k, half], x_to[half])
        for d in range(2):
            for half in (1 - d, d):
                part = partial(k, 3 if d else 1, half)
                if half == d:
                    acc[k, d] = part
                else:
                    stage_b[k, d, half] = part.astype(BF16)
                    b_send(k, d, half)
        for half in range(2):
            own[k, half] = partial(k, 0, half)

    def b_send(k, d, half):
        send(stage_b.at[k, d, half], got_b.at[k, d, half], b_s.at[k, d, half], b_r.at[k, d, half], x_to[d])

    def second(k):
        for d in range(2):
            got(got_a.at[k, d], a_s.at[k, d], a_r.at[k, d])
            stage_b[k, d, d] = (acc[k, d] + got_a[k, d].astype(F32)).astype(BF16)
            b_send(k, d, d)

    def t_copy(k, half):
        return remote(
            t_send.at[k, half], t_got.at[k, c], t_s.at[k, half], t_r.at[k, c], (at(z, row_of(k, 0), half), x)
        )

    def third(k):
        for half in range(2):
            for d in (0, 1):
                got(got_b.at[k, d, half], b_s.at[k, d, half], b_r.at[k, d, half])
            total = own[k, half] + got_b[k, 0, half].astype(F32) + got_b[k, 1, half].astype(F32)
            t_send[k, half] = total.astype(BF16)
            home = row_of(k, 0) * 2 + half == yc

            @pl.when(jnp.logical_not(home))
            def _():
                t_copy(k, half).start()

            @pl.when(home)
            def _():
                t_got[k, half] = t_send[k, half]

    def g_copy(k, d):
        pair = res.at[pl.ds(plane(k) * PLANE + row_of(k, 0) * 2, 2)]
        return pair

    def fourth(k):
        for half in range(2):
            home = row_of(k, 0) * 2 + half == yc

            @pl.when(jnp.logical_not(home))
            def _():
                got(t_got.at[k, half], t_s.at[k, half], t_r.at[k, half])

        s = plane(k) * PLANE + row_of(k, 0) * 2
        for half in range(2):
            p = tables_s[yc, 2, s + half]
            res[s + half] = dot(maps_local[p], t_got[k, half], 0, 0).astype(BF16)
        for d in range(2):
            there = res.at[pl.ds(s, 2)]
            send(there, there, g_s.at[k, d], g_r.at[k, d], x_to[d])

    def far(k, d, hop):
        dx = -hop if d == 0 else hop
        return plane(k) * PLANE + row_of(k, dx) * 2

    def fifth(k):
        for d in range(2):
            s = far(k, d, 1)
            got(res.at[pl.ds(s, 2)], g_s.at[k, d], g_r.at[k, d])
            send(res.at[s + d], res.at[s + d], f_s.at[k, d], f_r.at[k, d], x_to[d])

    def sixth(k):
        for d in range(2):
            got(res.at[far(k, d, 2) + d], f_s.at[k, d], f_r.at[k, d])

    steps = (first, second, third, fourth, fifth, sixth)

    def wave(front, lag_from, lag_to):
        for n in range(lag_from, lag_to):
            if 0 <= front - n < NZ:
                steps[n](front - n)

    for t in range(5):
        wave(t, 0, 6)
    z_turn(3)
    for t in range(5, 7):
        wave(t, 0, 6)
    for d in range(2):
        for o in orbitals(d, 4):
            z_got(d, 4, o)
    for t in range(7, NZ + 6):
        wave(t, 0, 6)

    def put(p, _):
        out[p] = res[tables_s[yc, 3, x * (PAIRS // NX) + p]]
        return 0

    lax.fori_loop(0, PAIRS // NX, put, 0)

    for copy in sent:
        copy.wait_send()
    for k in range(NZ):
        for half in range(2):
            home = row_of(k, 0) * 2 + half == yc

            @pl.when(jnp.logical_not(home))
            def _():
                t_copy(k, half).wait_send()


def body(blocks, wanted, pair_local, pair_slot, pno_local, pno_remote):
    dom, slab = blocks.shape[1:]
    npno = pno_local.shape[-1]
    slot = pair_slot.reshape(PAIRS, 1)
    hit = (slot == jnp.arange(PAIRS, dtype=I32)[None, :]).astype(I32)
    first = jnp.sum(hit * pair_local.reshape(PAIRS, 1), axis=0)
    place = jnp.sum(hit * jnp.arange(PAIRS, dtype=I32)[:, None], axis=0)
    lines = jnp.stack([wanted.reshape(PAIRS), first, place, pair_slot.reshape(PAIRS)])
    table = jnp.pad(lines, ((0, 4), (0, 128 - PAIRS)))

    dma = pltpu.SemaphoreType.DMA
    square = (dom, npno)
    call = pl.pallas_call(
        kernel,
        out_shape=jax.ShapeDtypeStruct((PAIRS // NX, npno, npno), BF16),
        in_specs=[pl.BlockSpec(memory_space=pl.ANY)] * 4,
        out_specs=pl.BlockSpec(memory_space=pltpu.VMEM),
        scratch_shapes=[pltpu.VMEM((4, dom, slab), BF16)] * NZ
        + [
            pltpu.VMEM((PLANE, 4, dom, slab), BF16),
            pltpu.VMEM((PLANE, NZ) + square, BF16),
            pltpu.VMEM((PAIRS,) + square, BF16),
            pltpu.VMEM((PLANE, 8, 128), I32),
            pltpu.SMEM((PLANE, 8, 128), I32),
            pltpu.VMEM((NZ, 2) + square, BF16),
            pltpu.VMEM((NZ, 2) + square, BF16),
            pltpu.VMEM((NZ, 2, 2) + square, BF16),
            pltpu.VMEM((NZ, 2, 2) + square, BF16),
            pltpu.VMEM((NZ, 2) + square, F32),
            pltpu.VMEM((NZ, 2) + square, F32),
            pltpu.VMEM((NZ, 2) + square, BF16),
            pltpu.VMEM((NZ, 2) + square, BF16),
            pltpu.VMEM((PAIRS, npno, npno), BF16),
            dma((2, 4, 4)), dma((2, 4, 4)),
            dma((2, 2, 4)), dma((2, 2, 4)),
            dma((4, 4)), dma((4, 4)),
            dma((7,)), dma((7,)),
            dma((2, 2, 2)), dma((2, 2, 2)),
            dma((7,)), dma((7,)),
            dma((NZ, 2)), dma((NZ, 2)),
            dma((NZ, 2, 2)), dma((NZ, 2, 2)),
            dma((NZ, 2)), dma((NZ, 2)),
            dma((NZ, 2)), dma((NZ, 2)),
            dma((NZ, 2)), dma((NZ, 2)),
            dma((6,)),
        ],
        compiler_params=pltpu.CompilerParams(
            collective_id=0, has_side_effects=True, vmem_limit_bytes=56 * 1024 * 1024
        ),
        cost_estimate=pl.CostEstimate(
            flops=4 * PAIRS * dom * slab * npno, bytes_accessed=1 << 24, transcendentals=0
        ),
    )
    maps = pno_remote.reshape(NZ, PLANE, dom, npno)
    return call(blocks, maps, pno_local.reshape(PAIRS, dom, npno), table)[None]


def solution(mesh):
    in_specs = (
        P("owner", None, "aux"),
        P("owner", None, None),
        P("owner", None),
        P("owner", None),
        P("owner", None, None, None),
        P("owner", None, None, None),
    )
    out_specs = P("owner", "aux", None, None)
    return jax.shard_map(body, mesh=mesh, in_specs=in_specs, out_specs=out_specs, check_vma=False)
```

```python
import jax
import jax.numpy as jnp
from jax import lax
from jax.experimental import pallas as pl
from jax.experimental.pallas import tpu as pltpu
from jax.sharding import PartitionSpec as P

NX, NY, NZ = 4, 4, 8
PLANE = NY * 2
PAIRS = 64
BF16, F32, I32 = jnp.bfloat16, jnp.float32, jnp.int32
MESH = pl.DeviceIdType.MESH
OFFSETS = (0, -1, 1, -2, 2, -3, 3, 4)
STRIPE, PART = 64, 32
UNITS = (
    (0, 1, 0, 3, 3.35),
    (1, 2, 0, 3, 3.4),
    (2, 3, 0, 3, 3.55),
    (0, 3, 3, 4, 4.15),
    (3, 4, 0, 4, 4.55),
    (4, 5, 0, 4, 5.05),
    (5, 6, 0, 4, 6.05),
    (6, 7, 0, 4, 6.1),
    (7, 8, 0, 4, 7.05),
)
LAST = len(UNITS) - 1
LATER = (
    (6.2, 0, 7), (6.25, 1, 6), (6.26, 2, 5), (7.06, 2, 6), (7.07, 1, 7), (7.08, 2, 7), (7.1, 1, 8), (7.11, 2, 8),
)
DIRECT = (LAST,)


def dot(a, b, ca, cb):
    return lax.dot_general(a, b, (((ca,), (cb,)), ((), ())), preferred_element_type=F32)


def kernel(
    blocks, pno_remote, pno_local, table, final,
    col0, col1, col2, col3, col4, col5, col6, col7,
    rows0, rows1, rows2, rows3, maps, maps_local, tables, tables_s,
    stage_a, got_a, stage_b, got_b, acc, own, t_send, t_got, tmp, res, picked,
    z_s, z_r, y_s, y_r, c_s, c_r, q_s, q_r, m_s, m_r, n_s, n_r, w_s, w_r,
    a_s, a_r, b_s, b_r, t_s, t_r, f_s, f_r, local_s,
):
    rows = (rows0, rows1, rows2, rows3)
    cols = (col0, col1, col2, col3, col4, col5, col6, col7)
    me = lax.axis_index("owner")
    x = lax.axis_index("aux")
    z = lax.div(me, PLANE)
    yc = lax.rem(me, PLANE)
    y = lax.div(yc, 2)
    c = lax.rem(yc, 2)

    def around(v, step, n):
        return lax.rem(v + (step + n), n)

    def at(zz, yy, cc):
        return (zz * NY + yy) * 2 + cc

    z_to = [(at(around(z, d, NZ), y, c), x) for d in (1, -1)]
    y_to = [(at(z, around(y, d, NY), c), x) for d in (1, -1)]
    x_to = [(me, around(x, d, NX)) for d in (1, -1)]
    x_far = (me, around(x, 2, NX))
    mate = (at(z, y, 1 - c), x)
    turns = [(dy, dc) for dy in (0, -1, 1, 2) for dc in (0, 1)]
    peers = [around(y, dy, NY) * 2 + lax.rem(c + dc, 2) for dy, dc in turns]
    whose = [around(y, -dy, NY) * 2 + lax.rem(c + dc, 2) for dy, dc in turns]

    def plane(k):
        return around(z, OFFSETS[k], NZ)

    barrier = pltpu.get_barrier_semaphore()
    hello = z_to + x_to + [x_far] + [(z * PLANE + p, x) for p in peers[1:]]
    for device in hello:
        pl.semaphore_signal(barrier, inc=1, device_id=device, device_id_type=MESH)
    pl.semaphore_wait(barrier, len(hello))

    sent = []

    def remote(src, dst, s, r, device):
        return pltpu.make_async_remote_copy(
            src_ref=src, dst_ref=dst, send_sem=s, recv_sem=r, device_id=device, device_id_type=MESH
        )

    def send(src, dst, s, r, device):
        copy = remote(src, dst, s, r, device)
        copy.start()
        sent.append(copy)

    def got(dst, s, r):
        remote(dst, dst, s, r, mate).wait_recv()

    local = []

    def copy_in(src, dst):
        copy = pltpu.make_async_copy(src, dst, local_s.at[len(local)])
        copy.start()
        local.append(copy)

    def column(d, h):
        return 7 if h == 4 else 2 * h - 1 + d

    def orbitals(d, h):
        return range(4) if h < 4 else (range(2) if d == 0 else range(2, 4))

    def z_send(d, h, q):
        src = blocks if h == 1 else cols[column(d, h - 1)]
        send(src.at[q], cols[column(d, h)].at[q], z_s.at[d, h - 1, q], z_r.at[d, h - 1, q], z_to[d])

    def z_got(d, h, q):
        got(cols[column(d, h)].at[q], z_s.at[d, h - 1, q], z_r.at[d, h - 1, q])

    def y_send(d, h, q):
        src = blocks.at[q] if h == 1 else rows[1 + d].at[c, q]
        dst = rows[1 + d] if h == 1 else rows[3]
        send(src, dst.at[c, q], y_s.at[d, h - 1, q], y_r.at[d, h - 1, q], y_to[d])

    def y_got(d, h, q):
        got((rows[1 + d] if h == 1 else rows[3]).at[c, q], y_s.at[d, h - 1, q], y_r.at[d, h - 1, q])

    def c_send(m, q):
        src = blocks if m == 0 else rows[m].at[c]
        send(src.at[q], rows[m].at[c, q], c_s.at[m, q], c_r.at[m, q], mate)

    def stripe_of(who):
        return pl.ds(pl.multiple_of(who * STRIPE, STRIPE), STRIPE)

    stripe = stripe_of(x)

    def q_send(n):
        src = pno_remote.at[:, peers[n], stripe]
        send(src, maps.at[yc, :, stripe], q_s.at[n], q_r.at[n], (z * PLANE + peers[n], x))

    def m_ref(n, who):
        return maps.at[whose[n], :, stripe_of(who)]

    def m_send(n, d):
        there = m_ref(n, x)
        send(there, there, m_s.at[d, n], m_r.at[d, n], x_to[d])

    def m_turn(n, d):
        there = m_ref(n, around(x, -1 if d == 0 else 1, NX))
        got(there, m_s.at[d, n], m_r.at[d, n])
        if n % 2 == d:
            send(there, there, n_s.at[d, n], n_r.at[d, n], x_to[d])

    def m_last(n):
        d = n % 2
        got(m_ref(n, around(x, -2 if d == 0 else 2, NX)), n_s.at[d, n], n_r.at[d, n])

    for n in range(2):
        for d in range(2):
            z_send(d, 1, n if d == 0 else 3 - n)
    copy_in(pno_remote.at[:, yc, stripe], maps.at[yc, :, stripe])
    for n in range(1, PLANE - 2):
        q_send(n)
    for n in range(2):
        for d in range(2):
            y_send(d, 1, n if d == 0 else 3 - n)
    local[0].wait()
    for d in range(2):
        m_send(0, d)
    for q in range(4):
        c_send(0, q)

    for n in range(1, PLANE):
        send(table, tables.at[yc], w_s.at[n], w_r.at[n], (z * PLANE + peers[n], x))

    first_local = len(local)
    copy_in(table, tables.at[yc])
    copy_in(blocks, col0)
    copy_in(blocks, rows0.at[c])
    copy_in(pno_local, maps_local)

    def w_turn():
        for n in range(1, PLANE):
            got(tables.at[whose[n]], w_s.at[n], w_r.at[n])
        for copy in local[first_local:]:
            copy.wait()
        scalars = pltpu.make_async_copy(tables, tables_s, local_s.at[len(local)])
        scalars.start()
        scalars.wait()

    def q_turn(n):
        got(maps.at[whose[n], :, stripe], q_s.at[n], q_r.at[n])
        for d in range(2):
            m_send(n, d)

    def z_turn(d, h, o, n):
        z_got(d, h, o)
        if h == 1 and n < 2:
            z_send(d, 1, o + 2 if d == 0 else o - 2)
        if h < 4 and o in orbitals(d, h + 1):
            z_send(d, h + 1, o)

    def y_turn(d, h, o, n):
        y_got(d, h, o)
        if h == 1 and n < 2:
            y_send(d, 1, o + 2 if d == 0 else o - 2)
        if h == 1 and n >= 2:
            y_send(d, 2, o - 2 if d == 0 else o + 2)
        c_send(1 + d if h == 1 else 3, o)

    def c_turn(*which):
        for m in which:
            for q in range(4):
                got(rows[m].at[1 - c, q], c_s.at[m, q], c_r.at[m, q])

    def part_of(dx):
        return pl.ds(pl.multiple_of(around(x, dx, NX) * PART, PART), PART)

    def partial(k, n):
        s = plane(k) * PLANE + yc
        i = tables_s[peers[n], 1, s]
        j = tables_s[peers[n], 0, s]
        right = dot(maps[peers[n], plane(k)], cols[k][j], 0, 0).astype(BF16)
        return dot(right, rows[n // 2][around(c, n % 2, 2), i], 1, 1)

    def share_of(u):
        k, k_end, m, m_end, _ = UNITS[u]
        return pl.ds(k, k_end - k), pl.ds(m, m_end - m)

    def b_ref(ref, u, d, half):
        ks, ms = share_of(u)
        return ref.at[ks, d, half, ms]

    def b_send(u, d, half):
        send(b_ref(stage_b, u, d, half), b_ref(got_b, u, d, half), b_s.at[u, d, half], b_r.at[u, d, half], x_to[d])

    def a_ref(ref, u, half):
        ks, ms = share_of(u)
        return ref.at[ks, half, ms]

    def first(u):
        k0, k1, m0, m1, _ = UNITS[u]
        for k in range(k0, k1):
            for n in range(2 * m0, 2 * m1):
                half, m = n % 2, n // 2
                tmp[half] = partial(k, n)
                stage_a[k, half, m] = tmp[half, part_of(2)].astype(BF16)
                for d in range(2):
                    part = tmp[half, part_of(-1 if d else 1)]
                    if half == d and u not in DIRECT:
                        acc[k, d, m] = part
                    else:
                        stage_b[k, d, half, m] = part.astype(BF16)
                own[k, half, m] = tmp[half, part_of(0)]
        for half in range(2):
            device = x_far if u in DIRECT else x_to[half]
            send(a_ref(stage_a, u, half), a_ref(got_a, u, half), a_s.at[u, half], a_r.at[u, half], device)
        for d in range(2):
            b_send(u, d, 1 - d)
            if u in DIRECT:
                b_send(u, d, d)

    def second(u):
        if u in DIRECT:
            return
        k0, k1, m0, m1, _ = UNITS[u]
        for d in range(2):
            got(a_ref(got_a, u, d), a_s.at[u, d], a_r.at[u, d])
            for k in range(k0, k1):
                for m in range(m0, m1):
                    stage_b[k, d, d, m] = (acc[k, d, m] + got_a[k, d, m].astype(F32)).astype(BF16)
            b_send(u, d, d)

    def b_wait(u):
        for half in range(2):
            for d in range(2):
                got(b_ref(got_b, u, d, half), b_s.at[u, d, half], b_r.at[u, d, half])
            if u in DIRECT:
                got(a_ref(got_a, u, half), a_s.at[u, half], a_r.at[u, half])

    def third(k):
        for half in range(2):
            total = own[k, half]
            for d in range(2):
                total = total + got_b[k, d, half].astype(F32)
            if LAST in DIRECT and k == NZ - 1:
                total = total + got_a[k, half].astype(F32)
            t_send[k, half] = total.astype(BF16)
            for m in range(NY):
                n = 2 * m + half
                if n == 0:
                    t_got[k, yc] = t_send[k, 0, 0]
                else:
                    send(
                        t_send.at[k, half, m], t_got.at[k, yc], t_s.at[k, n], t_r.at[k, n],
                        (z * PLANE + peers[n], x),
                    )

    def fourth(k):
        for n in range(PLANE):
            if n:
                got(t_got.at[k, whose[n]], t_s.at[k, n], t_r.at[k, n])
            s = plane(k) * PLANE + whose[n]
            p = tables_s[yc, 2, s]
            res[s] = dot(t_got[k, whose[n]], maps_local[p], 1, 0).astype(BF16)

    def thirds(u):
        b_wait(u)
        if u == 3:
            for k in range(3):
                third(k)
        elif u > 3:
            third(UNITS[u][0])

    def fourths(u):
        for k in range(3) if u == 3 else range(UNITS[u][0], UNITS[u][1]) if u > 3 else ():
            fourth(k)

    events = []

    def when(time, what, *args):
        events.append((time, len(events), what, args))

    for n in range(4):
        for d in range(2):
            o = n if d == 0 else 3 - n
            for h in (1, 2, 3):
                when(2 * (h - 1) + 0.5 * (n + 1), z_turn, d, h, o, n)
            when(1 + 0.5 * (n + 1), y_turn, d, 1, o, n)
            if n < 2:
                when(3 + 0.5 * (n + 1), y_turn, d, 2, o, n)
                when(6.5 + 0.5 * n, z_turn, d, 4, o, n)
    when(1.1, w_turn)
    for n in range(PLANE):
        if n:
            when(0.4 + 0.1 * n if n < 6 else 1.2 + 0.1 * n, q_turn, n)
        for d in range(2):
            when(0.75 + 0.33 * n, m_turn, n, d)
        when(1.3 + 0.33 * n, m_last, n)
    for n in range(PLANE - 2, PLANE):
        when(0.97, q_send, n)
    when(1.6, c_turn, 0)
    when(3.3, c_turn, 1, 2)
    when(4.1, c_turn, 3)
    begin = [unit[-1] for unit in UNITS]
    for u in range(LAST + 1):
        when(begin[u], first, u)
        for after, what in enumerate((second, thirds, fourths), start=1):
            if u + after < 8:
                when(begin[u + after] + 0.001 * after, what, u)
    for time, what, u in LATER:
        when(time, (second, thirds, fourths)[what], u)
    for _, _, what, args in sorted(events, key=lambda e: e[:2]):
        what(*args)

    share = PAIRS // NX
    for dx in (2, 1, 3, 0):
        def pick(p, _):
            picked[dx, p] = res[tables_s[yc, 3, around(x, dx, NX) * share + p]]
            return 0

        lax.fori_loop(0, share, pick, 0)
        if dx:
            device = (me, around(x, dx, NX))
            send(picked.at[dx], final.at[:, part_of(0)], f_s.at[dx], f_r.at[dx], device)
        else:
            final[:, part_of(0)] = picked[0]
    for dx in (1, 3, 2):
        got(final.at[:, part_of(-dx)], f_s.at[dx], f_r.at[dx])

    for copy in sent:
        copy.wait_send()


def body(blocks, wanted, pair_local, pair_slot, pno_local, pno_remote):
    dom, slab = blocks.shape[1:]
    npno = pno_local.shape[-1]
    dma = pltpu.SemaphoreType.DMA
    square, strip = (dom, npno), (PART, dom)

    def pair_of(*shape):
        return [dma(shape), dma(shape)]

    call = pl.pallas_call(
        kernel,
        out_shape=jax.ShapeDtypeStruct((PAIRS // NX, npno, npno), BF16),
        in_specs=[pl.BlockSpec(memory_space=pl.ANY)] * 4,
        out_specs=pl.BlockSpec(memory_space=pltpu.VMEM),
        scratch_shapes=[pltpu.VMEM((4, dom, slab), BF16)] * NZ
        + [pltpu.VMEM((2, 4, dom, slab), BF16)] * NY
        + [
            pltpu.VMEM((PLANE, NZ) + square, BF16),
            pltpu.VMEM((PAIRS,) + square, BF16),
            pltpu.VMEM((PLANE, 8, 128), I32),
            pltpu.SMEM((PLANE, 8, 128), I32),
            pltpu.VMEM((NZ, 2, NY) + strip, BF16),
            pltpu.VMEM((NZ, 2, NY) + strip, BF16),
            pltpu.VMEM((NZ, 2, 2, NY) + strip, BF16),
            pltpu.VMEM((NZ, 2, 2, NY) + strip, BF16),
            pltpu.VMEM((NZ, 2, NY) + strip, F32),
            pltpu.VMEM((NZ, 2, NY) + strip, F32),
            pltpu.VMEM((NZ, 2, NY) + strip, BF16),
            pltpu.VMEM((NZ, PLANE) + strip, BF16),
            pltpu.VMEM((2, npno, dom), F32),
            pltpu.VMEM((PAIRS, PART, npno), BF16),
            pltpu.VMEM((NX, PAIRS // NX, PART, npno), BF16),
        ]
        + pair_of(2, 4, 4)
        + pair_of(2, 2, 4)
        + pair_of(4, 4)
        + pair_of(PLANE)
        + pair_of(2, PLANE)
        + pair_of(2, PLANE)
        + pair_of(PLANE)
        + pair_of(LAST + 1, 2)
        + pair_of(LAST + 1, 2, 2)
        + pair_of(NZ, PLANE)
        + pair_of(NX)
        + [dma((6,))],
        compiler_params=pltpu.CompilerParams(
            collective_id=0, has_side_effects=True, vmem_limit_bytes=56 * 1024 * 1024
        ),
        cost_estimate=pl.CostEstimate(
            flops=4 * PAIRS * dom * slab * npno, bytes_accessed=1 << 24, transcendentals=0
        ),
    )
    maps = pno_remote.reshape(NZ, PLANE, dom, npno)
    slot = pair_slot.reshape(PAIRS, 1)
    hit = (slot == jnp.arange(PAIRS, dtype=I32)[None, :]).astype(I32)
    first = jnp.sum(hit * pair_local.reshape(PAIRS, 1), axis=0)
    place = jnp.sum(hit * jnp.arange(PAIRS, dtype=I32)[:, None], axis=0)
    lines = jnp.stack([wanted.reshape(PAIRS), first, place, pair_slot.reshape(PAIRS)])
    table = jnp.pad(lines, ((0, 4), (0, 128 - PAIRS)))
    turned = call(blocks, maps, pno_local.reshape(PAIRS, dom, npno), table)
    return jnp.swapaxes(turned, 1, 2)[None]


def solution(mesh):
    in_specs = (
        P("owner", None, "aux"),
        P("owner", None, None),
        P("owner", None),
        P("owner", None),
        P("owner", None, None, None),
        P("owner", None, None, None),
    )
    out_specs = P("owner", "aux", None, None)
    return jax.shard_map(body, mesh=mesh, in_specs=in_specs, out_specs=out_specs, check_vma=False)
```

```python
import jax
import jax.numpy as jnp
from jax import lax
from jax.experimental import pallas as pl
from jax.experimental.pallas import tpu as pltpu
from jax.sharding import PartitionSpec as P

NX, NY, NZ = 4, 4, 8
PLANE = NY * 2
PAIRS = 64
BF16, F32, I32 = jnp.bfloat16, jnp.float32, jnp.int32
MESH = pl.DeviceIdType.MESH
OFFSETS = (0, -1, 1, -2, 2, -3, 3, 4)
STRIPE, PART = 64, 32
UNITS = (
    (0, 1, 0, 3, 3.35),
    (1, 2, 0, 3, 3.4),
    (2, 3, 0, 3, 3.55),
    (0, 3, 3, 4, 4.15),
    (3, 4, 0, 4, 4.55),
    (4, 5, 0, 4, 5.05),
    (5, 6, 0, 4, 6.05),
    (6, 7, 0, 4, 6.1),
    (7, 8, 0, 4, 7.05),
)
LAST = len(UNITS) - 1
LATER = (
    (6.2, 0, 7), (6.25, 1, 6), (6.26, 2, 5), (7.06, 2, 6), (7.07, 1, 7), (7.1, 1, 8), (7.105, 2, 7), (7.11, 2, 8),
)
DIRECT = (LAST,)


def dot(a, b, ca, cb):
    return lax.dot_general(a, b, (((ca,), (cb,)), ((), ())), preferred_element_type=F32)


def kernel(
    blocks, pno_remote, pno_local, wanted, pair_local, pair_slot, final,
    col0, col1, col2, col3, col4, col5, col6, col7,
    rows0, rows1, rows2, rows3, maps, maps_local, table, tables, tables_s,
    stage_a, got_a, stage_b, got_b, acc, own, t_send, t_got, tmp, res, picked,
    z_s, z_r, y_s, y_r, c_s, c_r, q_s, q_r, m_s, m_r, n_s, n_r, w_s, w_r,
    a_s, a_r, b_s, b_r, t_s, t_r, f_s, f_r, local_s,
):
    rows = (rows0, rows1, rows2, rows3)
    cols = (col0, col1, col2, col3, col4, col5, col6, col7)
    me = lax.axis_index("owner")
    x = lax.axis_index("aux")
    z = lax.div(me, PLANE)
    yc = lax.rem(me, PLANE)
    y = lax.div(yc, 2)
    c = lax.rem(yc, 2)

    def around(v, step, n):
        return lax.rem(v + (step + n), n)

    def at(zz, yy, cc):
        return (zz * NY + yy) * 2 + cc

    z_to = [(at(around(z, d, NZ), y, c), x) for d in (1, -1)]
    y_to = [(at(z, around(y, d, NY), c), x) for d in (1, -1)]
    x_to = [(me, around(x, d, NX)) for d in (1, -1)]
    x_far = (me, around(x, 2, NX))
    mate = (at(z, y, 1 - c), x)
    turns = [(dy, dc) for dy in (0, -1, 1, 2) for dc in (0, 1)]
    peers = [around(y, dy, NY) * 2 + lax.rem(c + dc, 2) for dy, dc in turns]
    whose = [around(y, -dy, NY) * 2 + lax.rem(c + dc, 2) for dy, dc in turns]

    def plane(k):
        return around(z, OFFSETS[k], NZ)

    barrier = pltpu.get_barrier_semaphore()
    hello = z_to + x_to + [x_far] + [(z * PLANE + p, x) for p in peers[1:]]
    for device in hello:
        pl.semaphore_signal(barrier, inc=1, device_id=device, device_id_type=MESH)
    pl.semaphore_wait(barrier, len(hello))

    sent = []

    def remote(src, dst, s, r, device):
        return pltpu.make_async_remote_copy(
            src_ref=src, dst_ref=dst, send_sem=s, recv_sem=r, device_id=device, device_id_type=MESH
        )

    def send(src, dst, s, r, device):
        copy = remote(src, dst, s, r, device)
        copy.start()
        sent.append(copy)

    def got(dst, s, r):
        remote(dst, dst, s, r, mate).wait_recv()

    local = []

    def copy_in(src, dst):
        copy = pltpu.make_async_copy(src, dst, local_s.at[len(local)])
        copy.start()
        local.append(copy)

    def column(d, h):
        return 7 if h == 4 else 2 * h - 1 + d

    def orbitals(d, h):
        return range(4) if h < 4 else (range(2) if d == 0 else range(2, 4))

    def z_send(d, h, q):
        src = blocks if h == 1 else cols[column(d, h - 1)]
        send(src.at[q], cols[column(d, h)].at[q], z_s.at[d, h - 1, q], z_r.at[d, h - 1, q], z_to[d])

    def z_got(d, h, q):
        got(cols[column(d, h)].at[q], z_s.at[d, h - 1, q], z_r.at[d, h - 1, q])

    def y_send(d, h, q):
        src = blocks.at[q] if h == 1 else rows[1 + d].at[c, q]
        dst = rows[1 + d] if h == 1 else rows[3]
        send(src, dst.at[c, q], y_s.at[d, h - 1, q], y_r.at[d, h - 1, q], y_to[d])

    def y_got(d, h, q):
        got((rows[1 + d] if h == 1 else rows[3]).at[c, q], y_s.at[d, h - 1, q], y_r.at[d, h - 1, q])

    def c_send(m, q):
        src = blocks if m == 0 else rows[m].at[c]
        send(src.at[q], rows[m].at[c, q], c_s.at[m, q], c_r.at[m, q], mate)

    def stripe_of(who):
        return pl.ds(pl.multiple_of(who * STRIPE, STRIPE), STRIPE)

    stripe = stripe_of(x)

    def q_send(n):
        src = pno_remote.at[:, peers[n], stripe]
        send(src, maps.at[yc, :, stripe], q_s.at[n], q_r.at[n], (z * PLANE + peers[n], x))

    def m_ref(n, who):
        return maps.at[whose[n], :, stripe_of(who)]

    def m_send(n, d):
        there = m_ref(n, x)
        send(there, there, m_s.at[d, n], m_r.at[d, n], x_to[d])

    def m_turn(n, d):
        there = m_ref(n, around(x, -1 if d == 0 else 1, NX))
        got(there, m_s.at[d, n], m_r.at[d, n])
        if n % 2 == d:
            send(there, there, n_s.at[d, n], n_r.at[d, n], x_to[d])

    def m_last(n):
        d = n % 2
        got(m_ref(n, around(x, -2 if d == 0 else 2, NX)), n_s.at[d, n], n_r.at[d, n])

    for n in range(2):
        for d in range(2):
            z_send(d, 1, n if d == 0 else 3 - n)
    copy_in(pno_remote.at[:, yc, stripe], maps.at[yc, :, stripe])
    for n in range(1, PLANE - 2):
        q_send(n)
    for n in range(2):
        for d in range(2):
            y_send(d, 1, n if d == 0 else 3 - n)
    local[0].wait()
    for d in range(2):
        m_send(0, d)
    for q in range(4):
        c_send(0, q)

    ones = lax.broadcasted_iota(I32, (PAIRS, PAIRS), 0)
    lanes = lax.broadcasted_iota(I32, (PAIRS, PAIRS), 1)
    eye = (ones == lanes).astype(F32)
    slot = jnp.sum(eye * pair_slot[...].astype(F32), axis=1, keepdims=True)
    start = jnp.sum(eye * pair_local[...].astype(F32), axis=1, keepdims=True)
    hit = (slot.astype(I32) == lanes).astype(F32)
    table[...] = jnp.zeros_like(table)
    table[0:1, 0:PAIRS] = wanted[...]
    table[1:2, 0:PAIRS] = jnp.clip(jnp.max(hit * start, axis=0, keepdims=True).astype(I32), 0, 3)
    table[2:3, 0:PAIRS] = jnp.clip(
        jnp.max(hit * ones.astype(F32), axis=0, keepdims=True).astype(I32), 0, PAIRS - 1
    )
    table[3:4, 0:PAIRS] = pair_slot[...]
    for n in range(1, PLANE):
        send(table, tables.at[yc], w_s.at[n], w_r.at[n], (z * PLANE + peers[n], x))

    first_local = len(local)
    copy_in(table, tables.at[yc])
    copy_in(blocks, col0)
    copy_in(blocks, rows0.at[c])
    copy_in(pno_local, maps_local)

    def w_turn():
        for n in range(1, PLANE):
            got(tables.at[whose[n]], w_s.at[n], w_r.at[n])
        for copy in local[first_local:]:
            copy.wait()
        scalars = pltpu.make_async_copy(tables, tables_s, local_s.at[len(local)])
        scalars.start()
        scalars.wait()

    def q_turn(n):
        got(maps.at[whose[n], :, stripe], q_s.at[n], q_r.at[n])
        for d in range(2):
            m_send(n, d)

    def z_turn(d, h, o, n):
        z_got(d, h, o)
        if h == 1 and n < 2:
            z_send(d, 1, o + 2 if d == 0 else o - 2)
        if h < 4 and o in orbitals(d, h + 1):
            z_send(d, h + 1, o)

    def y_turn(d, h, o, n):
        y_got(d, h, o)
        if h == 1 and n < 2:
            y_send(d, 1, o + 2 if d == 0 else o - 2)
        if h == 1 and n >= 2:
            y_send(d, 2, o - 2 if d == 0 else o + 2)
        c_send(1 + d if h == 1 else 3, o)

    def c_turn(*which):
        for m in which:
            for q in range(4):
                got(rows[m].at[1 - c, q], c_s.at[m, q], c_r.at[m, q])

    def part_of(dx):
        return pl.ds(pl.multiple_of(around(x, dx, NX) * PART, PART), PART)

    def partial(k, n):
        s = plane(k) * PLANE + yc
        i = tables_s[peers[n], 1, s]
        j = tables_s[peers[n], 0, s]
        right = dot(maps[peers[n], plane(k)], cols[k][j], 0, 0).astype(BF16)
        return dot(right, rows[n // 2][around(c, n % 2, 2), i], 1, 1)

    def share_of(u):
        k, k_end, m, m_end, _ = UNITS[u]
        return pl.ds(k, k_end - k), pl.ds(m, m_end - m)

    def b_ref(ref, u, d, half):
        ks, ms = share_of(u)
        return ref.at[ks, d, half, ms]

    def b_send(u, d, half):
        send(b_ref(stage_b, u, d, half), b_ref(got_b, u, d, half), b_s.at[u, d, half], b_r.at[u, d, half], x_to[d])

    def a_ref(ref, u, half):
        ks, ms = share_of(u)
        return ref.at[ks, half, ms]

    def first(u):
        k0, k1, m0, m1, _ = UNITS[u]
        for k in range(k0, k1):
            for n in range(2 * m0, 2 * m1):
                half, m = n % 2, n // 2
                tmp[half] = partial(k, n)
                stage_a[k, half, m] = tmp[half, part_of(2)].astype(BF16)
                for d in range(2):
                    part = tmp[half, part_of(-1 if d else 1)]
                    if half == d and u not in DIRECT:
                        acc[k, d, m] = part
                    else:
                        stage_b[k, d, half, m] = part.astype(BF16)
                own[k, half, m] = tmp[half, part_of(0)]
        for half in range(2):
            device = x_far if u in DIRECT else x_to[half]
            send(a_ref(stage_a, u, half), a_ref(got_a, u, half), a_s.at[u, half], a_r.at[u, half], device)
        for d in range(2):
            b_send(u, d, 1 - d)
            if u in DIRECT:
                b_send(u, d, d)

    def second(u):
        if u in DIRECT:
            return
        k0, k1, m0, m1, _ = UNITS[u]
        for d in range(2):
            got(a_ref(got_a, u, d), a_s.at[u, d], a_r.at[u, d])
            for k in range(k0, k1):
                for m in range(m0, m1):
                    stage_b[k, d, d, m] = (acc[k, d, m] + got_a[k, d, m].astype(F32)).astype(BF16)
            b_send(u, d, d)

    def b_wait(u):
        for half in range(2):
            for d in range(2):
                got(b_ref(got_b, u, d, half), b_s.at[u, d, half], b_r.at[u, d, half])
            if u in DIRECT:
                got(a_ref(got_a, u, half), a_s.at[u, half], a_r.at[u, half])

    def third(k):
        for half in range(2):
            total = own[k, half]
            for d in range(2):
                total = total + got_b[k, d, half].astype(F32)
            if LAST in DIRECT and k == NZ - 1:
                total = total + got_a[k, half].astype(F32)
            t_send[k, half] = total.astype(BF16)
            for m in range(NY):
                n = 2 * m + half
                if n == 0:
                    t_got[k, yc] = t_send[k, 0, 0]
                else:
                    send(
                        t_send.at[k, half, m], t_got.at[k, yc], t_s.at[k, n], t_r.at[k, n],
                        (z * PLANE + peers[n], x),
                    )

    def fourth(k):
        for n in range(PLANE):
            if n:
                got(t_got.at[k, whose[n]], t_s.at[k, n], t_r.at[k, n])
            s = plane(k) * PLANE + whose[n]
            p = tables_s[yc, 2, s]
            res[s] = dot(t_got[k, whose[n]], maps_local[p], 1, 0).astype(BF16)

    def thirds(u):
        b_wait(u)
        if u == 3:
            for k in range(3):
                third(k)
        elif u > 3:
            third(UNITS[u][0])

    def fourths(u):
        for k in range(3) if u == 3 else range(UNITS[u][0], UNITS[u][1]) if u > 3 else ():
            fourth(k)

    events = []

    def when(time, what, *args):
        events.append((time, len(events), what, args))

    for n in range(4):
        for d in range(2):
            o = n if d == 0 else 3 - n
            for h in (1, 2, 3):
                when(2 * (h - 1) + 0.5 * (n + 1), z_turn, d, h, o, n)
            when(1 + 0.5 * (n + 1), y_turn, d, 1, o, n)
            if n < 2:
                when(3 + 0.5 * (n + 1), y_turn, d, 2, o, n)
                when(6.5 + 0.5 * n, z_turn, d, 4, o, n)
    when(1.1, w_turn)
    for n in range(PLANE):
        if n:
            when(0.4 + 0.1 * n if n < 6 else 1.2 + 0.1 * n, q_turn, n)
        for d in range(2):
            when(0.75 + 0.33 * n, m_turn, n, d)
        when(1.3 + 0.33 * n, m_last, n)
    for n in range(PLANE - 2, PLANE):
        when(0.97, q_send, n)
    when(1.6, c_turn, 0)
    when(3.3, c_turn, 1, 2)
    when(4.1, c_turn, 3)
    begin = [unit[-1] for unit in UNITS]
    for u in range(LAST + 1):
        when(begin[u], first, u)
        for after, what in enumerate((second, thirds, fourths), start=1):
            if u + after < 8:
                when(begin[u + after] + 0.001 * after, what, u)
    for time, what, u in LATER:
        when(time, (second, thirds, fourths)[what], u)
    for _, _, what, args in sorted(events, key=lambda e: e[:2]):
        what(*args)

    share = PAIRS // NX
    for dx in (2, 1, 3, 0):
        def pick(p, _):
            picked[dx, p] = res[tables_s[yc, 3, around(x, dx, NX) * share + p]]
            return 0

        lax.fori_loop(0, share, pick, 0)
        if dx:
            device = (me, around(x, dx, NX))
            send(picked.at[dx], final.at[:, part_of(0)], f_s.at[dx], f_r.at[dx], device)
        else:
            final[:, part_of(0)] = picked[0]
    for dx in (1, 3, 2):
        got(final.at[:, part_of(-dx)], f_s.at[dx], f_r.at[dx])

    for copy in sent:
        copy.wait_send()


def body(blocks, wanted, pair_local, pair_slot, pno_local, pno_remote):
    dom, slab = blocks.shape[1:]
    npno = pno_local.shape[-1]
    dma = pltpu.SemaphoreType.DMA
    square, strip = (dom, npno), (PART, dom)

    def pair_of(*shape):
        return [dma(shape), dma(shape)]

    call = pl.pallas_call(
        kernel,
        out_shape=jax.ShapeDtypeStruct((PAIRS // NX, npno, npno), BF16),
        in_specs=[pl.BlockSpec(memory_space=pl.ANY)] * 3 + [pl.BlockSpec(memory_space=pltpu.VMEM)] * 3,
        out_specs=pl.BlockSpec(memory_space=pltpu.VMEM),
        scratch_shapes=[pltpu.VMEM((4, dom, slab), BF16)] * NZ
        + [pltpu.VMEM((2, 4, dom, slab), BF16)] * NY
        + [
            pltpu.VMEM((PLANE, NZ) + square, BF16),
            pltpu.VMEM((PAIRS,) + square, BF16),
            pltpu.VMEM((8, 128), I32),
            pltpu.VMEM((PLANE, 8, 128), I32),
            pltpu.SMEM((PLANE, 8, 128), I32),
            pltpu.VMEM((NZ, 2, NY) + strip, BF16),
            pltpu.VMEM((NZ, 2, NY) + strip, BF16),
            pltpu.VMEM((NZ, 2, 2, NY) + strip, BF16),
            pltpu.VMEM((NZ, 2, 2, NY) + strip, BF16),
            pltpu.VMEM((NZ, 2, NY) + strip, F32),
            pltpu.VMEM((NZ, 2, NY) + strip, F32),
            pltpu.VMEM((NZ, 2, NY) + strip, BF16),
            pltpu.VMEM((NZ, PLANE) + strip, BF16),
            pltpu.VMEM((2, npno, dom), F32),
            pltpu.VMEM((PAIRS, PART, npno), BF16),
            pltpu.VMEM((NX, PAIRS // NX, PART, npno), BF16),
        ]
        + pair_of(2, 4, 4)
        + pair_of(2, 2, 4)
        + pair_of(4, 4)
        + pair_of(PLANE)
        + pair_of(2, PLANE)
        + pair_of(2, PLANE)
        + pair_of(PLANE)
        + pair_of(LAST + 1, 2)
        + pair_of(LAST + 1, 2, 2)
        + pair_of(NZ, PLANE)
        + pair_of(NX)
        + [dma((6,))],
        compiler_params=pltpu.CompilerParams(
            collective_id=0, has_side_effects=True, vmem_limit_bytes=56 * 1024 * 1024
        ),
        cost_estimate=pl.CostEstimate(
            flops=4 * PAIRS * dom * slab * npno, bytes_accessed=1 << 24, transcendentals=0
        ),
    )
    maps = pno_remote.reshape(NZ, PLANE, dom, npno)
    turned = call(
        blocks, maps, pno_local.reshape(PAIRS, dom, npno), wanted.reshape(1, PAIRS), pair_local, pair_slot
    )
    return jnp.swapaxes(turned, 1, 2)[None]


def solution(mesh):
    in_specs = (
        P("owner", None, "aux"),
        P("owner", None, None),
        P("owner", None),
        P("owner", None),
        P("owner", None, None, None),
        P("owner", None, None, None),
    )
    out_specs = P("owner", "aux", None, None)
    return jax.shard_map(body, mesh=mesh, in_specs=in_specs, out_specs=out_specs, check_vma=False)
```

```python
import jax
import jax.numpy as jnp
from jax import lax
from jax.experimental import pallas as pl
from jax.experimental.pallas import tpu as pltpu
from jax.sharding import PartitionSpec as P

NX, NY, NZ = 4, 4, 8
PLANE = NY * 2
PAIRS = 64
BF16, F32, I32 = jnp.bfloat16, jnp.float32, jnp.int32
MESH = pl.DeviceIdType.MESH
OFFSETS = (0, -1, 1, -2, 2, -3, 3, 4)
STRIPE, PART = 64, 32
UNITS = (
    (0, 1, 0, 3, 3.35),
    (1, 2, 0, 3, 3.4),
    (2, 3, 0, 3, 3.55),
    (0, 3, 3, 4, 4.15),
    (3, 4, 0, 4, 4.55),
    (4, 5, 0, 4, 5.05),
    (5, 6, 0, 4, 6.05),
    (6, 7, 0, 4, 6.1),
    (7, 8, 0, 4, 7.05),
)
LAST = len(UNITS) - 1
LATER = (
    (6.2, 0, 7), (6.25, 1, 6), (6.26, 2, 5), (7.06, 2, 6), (7.07, 1, 7), (7.1, 1, 8), (7.105, 2, 7), (7.11, 2, 8),
)
DIRECT = (LAST,)


def dot(a, b, ca, cb):
    return lax.dot_general(a, b, (((ca,), (cb,)), ((), ())), preferred_element_type=F32)


def kernel(
    blocks, pno_remote, pno_local, wanted, pair_local, pair_slot, final,
    col0, col1, col2, col3, col4, col5, col6, col7,
    rows0, rows1, rows2, rows3, maps, maps_local, table, tables, tables_s,
    stage_a, got_a, stage_b, got_b, acc, own, t_send, t_got, tmp, res, picked,
    z_s, z_r, y_s, y_r, c_s, c_r, q_s, q_r, m_s, m_r, n_s, n_r, w_s, w_r,
    a_s, a_r, b_s, b_r, t_s, t_r, f_s, f_r, local_s,
):
    rows = (rows0, rows1, rows2, rows3)
    cols = (col0, col1, col2, col3, col4, col5, col6, col7)
    me = lax.axis_index("owner")
    x = lax.axis_index("aux")
    z = lax.div(me, PLANE)
    yc = lax.rem(me, PLANE)
    y = lax.div(yc, 2)
    c = lax.rem(yc, 2)

    def around(v, step, n):
        return lax.rem(v + (step + n), n)

    def at(zz, yy, cc):
        return (zz * NY + yy) * 2 + cc

    z_to = [(at(around(z, d, NZ), y, c), x) for d in (1, -1)]
    y_to = [(at(z, around(y, d, NY), c), x) for d in (1, -1)]
    x_to = [(me, around(x, d, NX)) for d in (1, -1)]
    x_far = (me, around(x, 2, NX))
    mate = (at(z, y, 1 - c), x)
    turns = [(dy, dc) for dy in (0, -1, 1, 2) for dc in (0, 1)]
    peers = [around(y, dy, NY) * 2 + lax.rem(c + dc, 2) for dy, dc in turns]
    whose = [around(y, -dy, NY) * 2 + lax.rem(c + dc, 2) for dy, dc in turns]

    def plane(k):
        return around(z, OFFSETS[k], NZ)

    barrier = pltpu.get_barrier_semaphore()
    hello = z_to + x_to + [x_far] + [(z * PLANE + p, x) for p in peers[1:]]
    for device in hello:
        pl.semaphore_signal(barrier, inc=1, device_id=device, device_id_type=MESH)
    pl.semaphore_wait(barrier, len(hello))

    sent = []

    def remote(src, dst, s, r, device):
        return pltpu.make_async_remote_copy(
            src_ref=src, dst_ref=dst, send_sem=s, recv_sem=r, device_id=device, device_id_type=MESH
        )

    def send(src, dst, s, r, device):
        copy = remote(src, dst, s, r, device)
        copy.start()
        sent.append(copy)

    def got(dst, s, r):
        remote(dst, dst, s, r, mate).wait_recv()

    local = []

    def copy_in(src, dst):
        copy = pltpu.make_async_copy(src, dst, local_s.at[len(local)])
        copy.start()
        local.append(copy)

    def column(d, h):
        return 7 if h == 4 else 2 * h - 1 + d

    def orbitals(d, h):
        return range(4) if h < 4 else (range(2) if d == 0 else range(2, 4))

    def z_send(d, h, q):
        src = blocks if h == 1 else cols[column(d, h - 1)]
        send(src.at[q], cols[column(d, h)].at[q], z_s.at[d, h - 1, q], z_r.at[d, h - 1, q], z_to[d])

    def z_got(d, h, q):
        got(cols[column(d, h)].at[q], z_s.at[d, h - 1, q], z_r.at[d, h - 1, q])

    def y_send(d, h, q):
        src = blocks.at[q] if h == 1 else rows[1 + d].at[c, q]
        dst = rows[1 + d] if h == 1 else rows[3]
        send(src, dst.at[c, q], y_s.at[d, h - 1, q], y_r.at[d, h - 1, q], y_to[d])

    def y_got(d, h, q):
        got((rows[1 + d] if h == 1 else rows[3]).at[c, q], y_s.at[d, h - 1, q], y_r.at[d, h - 1, q])

    def c_send(m, q):
        src = blocks if m == 0 else rows[m].at[c]
        send(src.at[q], rows[m].at[c, q], c_s.at[m, q], c_r.at[m, q], mate)

    def stripe_of(who):
        return pl.ds(pl.multiple_of(who * STRIPE, STRIPE), STRIPE)

    stripe = stripe_of(x)

    def q_send(n):
        src = pno_remote.at[:, peers[n], stripe]
        send(src, maps.at[yc, :, stripe], q_s.at[n], q_r.at[n], (z * PLANE + peers[n], x))

    def m_ref(n, who):
        return maps.at[whose[n], :, stripe_of(who)]

    def m_send(n, d):
        there = m_ref(n, x)
        send(there, there, m_s.at[d, n], m_r.at[d, n], x_to[d])

    def m_turn(n, d):
        there = m_ref(n, around(x, -1 if d == 0 else 1, NX))
        got(there, m_s.at[d, n], m_r.at[d, n])
        if n % 2 == d:
            send(there, there, n_s.at[d, n], n_r.at[d, n], x_to[d])

    def m_last(n):
        d = n % 2
        got(m_ref(n, around(x, -2 if d == 0 else 2, NX)), n_s.at[d, n], n_r.at[d, n])

    for n in range(2):
        for d in range(2):
            z_send(d, 1, n if d == 0 else 3 - n)
    copy_in(pno_remote.at[:, yc, stripe], maps.at[yc, :, stripe])
    for n in range(1, PLANE - 2):
        q_send(n)
    for n in range(2):
        for d in range(2):
            y_send(d, 1, n if d == 0 else 3 - n)
    local[0].wait()
    for d in range(2):
        m_send(0, d)
    for q in range(4):
        c_send(0, q)

    ones = lax.broadcasted_iota(I32, (PAIRS, PAIRS), 0)
    lanes = lax.broadcasted_iota(I32, (PAIRS, PAIRS), 1)
    eye = (ones == lanes).astype(F32)
    slot = jnp.sum(eye * pair_slot[...].astype(F32), axis=1, keepdims=True)
    start = jnp.sum(eye * pair_local[...].astype(F32), axis=1, keepdims=True)
    hit = (slot.astype(I32) == lanes).astype(F32)
    table[...] = jnp.zeros_like(table)
    table[0:1, 0:PAIRS] = wanted[...]
    table[1:2, 0:PAIRS] = jnp.clip(jnp.max(hit * start, axis=0, keepdims=True).astype(I32), 0, 3)
    table[2:3, 0:PAIRS] = jnp.clip(
        jnp.max(hit * ones.astype(F32), axis=0, keepdims=True).astype(I32), 0, PAIRS - 1
    )
    table[3:4, 0:PAIRS] = pair_slot[...]
    for n in range(1, PLANE):
        send(table, tables.at[yc], w_s.at[n], w_r.at[n], (z * PLANE + peers[n], x))

    first_local = len(local)
    copy_in(table, tables.at[yc])
    copy_in(blocks, col0)
    copy_in(blocks, rows0.at[c])
    copy_in(pno_local, maps_local)

    def w_turn():
        for n in range(1, PLANE):
            got(tables.at[whose[n]], w_s.at[n], w_r.at[n])
        for copy in local[first_local:]:
            copy.wait()
        scalars = pltpu.make_async_copy(tables, tables_s, local_s.at[len(local)])
        scalars.start()
        scalars.wait()

    def q_turn(n):
        got(maps.at[whose[n], :, stripe], q_s.at[n], q_r.at[n])
        for d in range(2):
            m_send(n, d)

    def z_turn(d, h, o, n):
        z_got(d, h, o)
        if h == 1 and n < 2:
            z_send(d, 1, o + 2 if d == 0 else o - 2)
        if h < 4 and o in orbitals(d, h + 1):
            z_send(d, h + 1, o)

    def y_turn(d, h, o, n):
        y_got(d, h, o)
        if h == 1 and n < 2:
            y_send(d, 1, o + 2 if d == 0 else o - 2)
        if h == 1 and n >= 2:
            y_send(d, 2, o - 2 if d == 0 else o + 2)
        c_send(1 + d if h == 1 else 3, o)

    def c_turn(*which):
        for m in which:
            for q in range(4):
                got(rows[m].at[1 - c, q], c_s.at[m, q], c_r.at[m, q])

    def part_of(dx):
        return pl.ds(pl.multiple_of(around(x, dx, NX) * PART, PART), PART)

    def partial(k, n):
        s = plane(k) * PLANE + yc
        i = tables_s[peers[n], 1, s]
        j = tables_s[peers[n], 0, s]
        right = dot(maps[peers[n], plane(k)], cols[k][j], 0, 0).astype(BF16)
        return dot(right, rows[n // 2][around(c, n % 2, 2), i], 1, 1)

    def share_of(u):
        k, k_end, m, m_end, _ = UNITS[u]
        return pl.ds(k, k_end - k), pl.ds(m, m_end - m)

    def b_ref(ref, u, d, half):
        ks, ms = share_of(u)
        return ref.at[ks, d, half, ms]

    def b_send(u, d, half):
        send(b_ref(stage_b, u, d, half), b_ref(got_b, u, d, half), b_s.at[u, d, half], b_r.at[u, d, half], x_to[d])

    def a_ref(ref, u, half):
        ks, ms = share_of(u)
        return ref.at[ks, half, ms]

    def first(u):
        k0, k1, m0, m1, _ = UNITS[u]
        for half in range(2):
            for k in range(k0, k1):
                for m in range(m0, m1):
                    slot = m % 2
                    tmp[slot] = partial(k, 2 * m + half)
                    stage_a[k, half, m] = tmp[slot, part_of(2)].astype(BF16)
                    for d in range(2):
                        part = tmp[slot, part_of(-1 if d else 1)]
                        if half == d and u not in DIRECT:
                            acc[k, d, m] = part
                        else:
                            stage_b[k, d, half, m] = part.astype(BF16)
                    own[k, half, m] = tmp[slot, part_of(0)]
            device = x_far if u in DIRECT else x_to[half]
            send(a_ref(stage_a, u, half), a_ref(got_a, u, half), a_s.at[u, half], a_r.at[u, half], device)
            b_send(u, 1 - half, half)
            if u in DIRECT:
                b_send(u, half, half)

    def second(u):
        if u in DIRECT:
            return
        k0, k1, m0, m1, _ = UNITS[u]
        for d in range(2):
            got(a_ref(got_a, u, d), a_s.at[u, d], a_r.at[u, d])
            for k in range(k0, k1):
                for m in range(m0, m1):
                    stage_b[k, d, d, m] = (acc[k, d, m] + got_a[k, d, m].astype(F32)).astype(BF16)
            b_send(u, d, d)

    def b_wait(u):
        for half in range(2):
            for d in range(2):
                got(b_ref(got_b, u, d, half), b_s.at[u, d, half], b_r.at[u, d, half])
            if u in DIRECT:
                got(a_ref(got_a, u, half), a_s.at[u, half], a_r.at[u, half])

    def third(k):
        for half in range(2):
            total = own[k, half]
            for d in range(2):
                total = total + got_b[k, d, half].astype(F32)
            if LAST in DIRECT and k == NZ - 1:
                total = total + got_a[k, half].astype(F32)
            t_send[k, half] = total.astype(BF16)
            for m in range(NY):
                n = 2 * m + half
                if n == 0:
                    t_got[k, yc] = t_send[k, 0, 0]
                else:
                    send(
                        t_send.at[k, half, m], t_got.at[k, yc], t_s.at[k, n], t_r.at[k, n],
                        (z * PLANE + peers[n], x),
                    )

    def fourth(k):
        for n in range(PLANE):
            if n:
                got(t_got.at[k, whose[n]], t_s.at[k, n], t_r.at[k, n])
            s = plane(k) * PLANE + whose[n]
            p = tables_s[yc, 2, s]
            res[s] = dot(t_got[k, whose[n]], maps_local[p], 1, 0).astype(BF16)

    def thirds(u):
        b_wait(u)
        if u == 3:
            for k in range(3):
                third(k)
        elif u > 3:
            third(UNITS[u][0])

    def fourths(u):
        for k in range(3) if u == 3 else range(UNITS[u][0], UNITS[u][1]) if u > 3 else ():
            fourth(k)

    events = []

    def when(time, what, *args):
        events.append((time, len(events), what, args))

    for n in range(4):
        for d in range(2):
            o = n if d == 0 else 3 - n
            for h in (1, 2, 3):
                when(2 * (h - 1) + 0.5 * (n + 1), z_turn, d, h, o, n)
            when(1 + 0.5 * (n + 1), y_turn, d, 1, o, n)
            if n < 2:
                when(3 + 0.5 * (n + 1), y_turn, d, 2, o, n)
                when(6.5 + 0.5 * n, z_turn, d, 4, o, n)
    when(1.1, w_turn)
    for n in range(PLANE):
        if n:
            when(0.4 + 0.1 * n if n < 6 else 1.2 + 0.1 * n, q_turn, n)
        for d in range(2):
            when(0.75 + 0.33 * n, m_turn, n, d)
        when(1.3 + 0.33 * n, m_last, n)
    for n in range(PLANE - 2, PLANE):
        when(0.97, q_send, n)
    when(1.6, c_turn, 0)
    when(3.3, c_turn, 1, 2)
    when(4.1, c_turn, 3)
    begin = [unit[-1] for unit in UNITS]
    for u in range(LAST + 1):
        when(begin[u], first, u)
        for after, what in enumerate((second, thirds, fourths), start=1):
            if u + after < 8:
                when(begin[u + after] + 0.001 * after, what, u)
    for time, what, u in LATER:
        when(time, (second, thirds, fourths)[what], u)
    for _, _, what, args in sorted(events, key=lambda e: e[:2]):
        what(*args)

    share = PAIRS // NX
    for dx in (2, 1, 3, 0):
        def pick(p, _):
            picked[dx, p] = res[tables_s[yc, 3, around(x, dx, NX) * share + p]]
            return 0

        lax.fori_loop(0, share, pick, 0)
        if dx:
            device = (me, around(x, dx, NX))
            send(picked.at[dx], final.at[:, part_of(0)], f_s.at[dx], f_r.at[dx], device)
        else:
            final[:, part_of(0)] = picked[0]
    for dx in (1, 3, 2):
        got(final.at[:, part_of(-dx)], f_s.at[dx], f_r.at[dx])

    for copy in sent:
        copy.wait_send()


def body(blocks, wanted, pair_local, pair_slot, pno_local, pno_remote):
    dom, slab = blocks.shape[1:]
    npno = pno_local.shape[-1]
    dma = pltpu.SemaphoreType.DMA
    square, strip = (dom, npno), (PART, dom)

    def pair_of(*shape):
        return [dma(shape), dma(shape)]

    call = pl.pallas_call(
        kernel,
        out_shape=jax.ShapeDtypeStruct((PAIRS // NX, npno, npno), BF16),
        in_specs=[pl.BlockSpec(memory_space=pl.ANY)] * 3 + [pl.BlockSpec(memory_space=pltpu.VMEM)] * 3,
        out_specs=pl.BlockSpec(memory_space=pltpu.VMEM),
        scratch_shapes=[pltpu.VMEM((4, dom, slab), BF16)] * NZ
        + [pltpu.VMEM((2, 4, dom, slab), BF16)] * NY
        + [
            pltpu.VMEM((PLANE, NZ) + square, BF16),
            pltpu.VMEM((PAIRS,) + square, BF16),
            pltpu.VMEM((8, 128), I32),
            pltpu.VMEM((PLANE, 8, 128), I32),
            pltpu.SMEM((PLANE, 8, 128), I32),
            pltpu.VMEM((NZ, 2, NY) + strip, BF16),
            pltpu.VMEM((NZ, 2, NY) + strip, BF16),
            pltpu.VMEM((NZ, 2, 2, NY) + strip, BF16),
            pltpu.VMEM((NZ, 2, 2, NY) + strip, BF16),
            pltpu.VMEM((NZ, 2, NY) + strip, F32),
            pltpu.VMEM((NZ, 2, NY) + strip, F32),
            pltpu.VMEM((NZ, 2, NY) + strip, BF16),
            pltpu.VMEM((NZ, PLANE) + strip, BF16),
            pltpu.VMEM((2, npno, dom), F32),
            pltpu.VMEM((PAIRS, PART, npno), BF16),
            pltpu.VMEM((NX, PAIRS // NX, PART, npno), BF16),
        ]
        + pair_of(2, 4, 4)
        + pair_of(2, 2, 4)
        + pair_of(4, 4)
        + pair_of(PLANE)
        + pair_of(2, PLANE)
        + pair_of(2, PLANE)
        + pair_of(PLANE)
        + pair_of(LAST + 1, 2)
        + pair_of(LAST + 1, 2, 2)
        + pair_of(NZ, PLANE)
        + pair_of(NX)
        + [dma((6,))],
        compiler_params=pltpu.CompilerParams(
            collective_id=0, has_side_effects=True, vmem_limit_bytes=56 * 1024 * 1024
        ),
        cost_estimate=pl.CostEstimate(
            flops=4 * PAIRS * dom * slab * npno, bytes_accessed=1 << 24, transcendentals=0
        ),
    )
    maps = pno_remote.reshape(NZ, PLANE, dom, npno)
    turned = call(
        blocks, maps, pno_local.reshape(PAIRS, dom, npno), wanted.reshape(1, PAIRS), pair_local, pair_slot
    )
    return jnp.swapaxes(turned, 1, 2)[None]


def solution(mesh):
    in_specs = (
        P("owner", None, "aux"),
        P("owner", None, None),
        P("owner", None),
        P("owner", None),
        P("owner", None, None, None),
        P("owner", None, None, None),
    )
    out_specs = P("owner", "aux", None, None)
    return jax.shard_map(body, mesh=mesh, in_specs=in_specs, out_specs=out_specs, check_vma=False)
```
